256 devices in a mesh: in: 8 (over x, z_lo), out: 32 (over y, z_hi, core).
Axes of the slice: x: 4, y: 4, z: 8 (z_hi: 4, z_lo: 2; z = z_hi * 2 + z_lo), core: 2. Of those that a mesh axis runs over, the one named last changes fastest.
Arguments:
- activations: bfloat16 [4096, 8192], P('out', 'in'), may hold values from -6 to 6
- cotangent: bfloat16 [4096, 28672], P('in', 'out'), may hold values from -0.09375 to 0.09375
- basis_in: float32 [8192, 512], P('in'), may hold values from -1 to 1, as said below
- basis_out: float32 [28672, 1024], P('out'), may hold values from -1 to 1, as said below
Outputs:
- projected: float32 [8192, 28672], P('in', 'out')
The draws below stay inside these ranges and needn't reach their ends.
Inputs may be any that keep to these rules, and one draw needn't show every extreme that they name: The columns of basis_in are orthonormal. The columns of basis_out are orthonormal.
All inputs are finite; a program needn't handle non-finite values.
Results may differ from the reference program's by a relative error of at most 0.0003.
Values may be sent and summed in bfloat16 or wider, within the bound.
No kernel may reach another device: no remote copies, remote signals or barrier semaphores. Data moves between devices by JAX's collectives and lax.ppermute only.
A program may use at most 128 MiB of HBM per device.

```python
import math
import jax
import jax.numpy as jnp
from jax import lax

D = 8192
FF = 28672
RU = 512
RV = 1024
TOKENS = 4096


def orthonormal_columns(key, row_count, col_count):
    power_two = row_count & -row_count
    odd_factor = row_count // power_two
    bit_count = power_two.bit_length() - 1
    first_key, second_key, third_key = jax.random.split(key, 3)
    chosen = jax.random.permutation(first_key, row_count)[:col_count].astype(jnp.int32)
    col_outer = chosen // power_two
    col_inner = chosen % power_two
    row_ids = jnp.arange(row_count, dtype=jnp.int32)
    row_outer = row_ids // power_two
    row_inner = row_ids % power_two
    common = jnp.bitwise_and(row_inner[:, None], col_inner[None, :])
    parity = jnp.zeros((row_count, col_count), jnp.int32)
    for level in range(bit_count):
        parity = parity + jnp.bitwise_and(jnp.right_shift(common, level), 1)
    walsh = 1.0 - 2.0 * (parity % 2).astype(jnp.float32)
    frequency = col_outer.astype(jnp.float32)[None, :]
    position = row_outer.astype(jnp.float32)[:, None]
    weighting = jnp.where(frequency == 0.0, math.sqrt(1.0 / odd_factor), math.sqrt(2.0 / odd_factor))
    cosine = jnp.cos(math.pi * (2.0 * position + 1.0) * frequency / (2.0 * odd_factor)) * weighting
    row_signs = 1.0 - 2.0 * jax.random.randint(second_key, (row_count,), 0, 2).astype(jnp.float32)
    columns = row_signs[:, None] * cosine * walsh / math.sqrt(power_two)
    angles = jax.random.uniform(third_key, (col_count // 2,), jnp.float32, -math.pi, math.pi)
    paired = columns.reshape(row_count, col_count // 2, 2)
    first_col = paired[:, :, 0]
    second_col = paired[:, :, 1]
    cosines = jnp.cos(angles)[None, :]
    sines = jnp.sin(angles)[None, :]
    rotated = jnp.stack([cosines * first_col - sines * second_col, sines * first_col + cosines * second_col], axis=-1)
    return rotated.reshape(row_count, col_count).astype(jnp.float32)


def draw_basis_in(key, part):
    key = jax.random.fold_in(key, 11)
    return orthonormal_columns(key, D, RU)


def draw_basis_out(key, part):
    key = jax.random.fold_in(key, 12)
    return orthonormal_columns(key, FF, RV)


def levels(key, extent, cuts, low, largest):
    def one(dim, blocks):
        steps = jax.random.uniform(jax.random.fold_in(jax.random.fold_in(key, 6), dim), (blocks,), jnp.float32, low / len(cuts), largest / len(cuts))
        return jnp.repeat(jnp.exp(steps), extent[dim] // blocks).reshape((-1,) + (1,) * (len(extent) - dim - 1))

    gain = one(*cuts[0])
    for cut in cuts[1:]:
        gain = gain * one(*cut)
    return gain


def noise(rng, dims, deviation, reach, pieces=(), kind=jnp.bfloat16):
    loudness = levels(rng, dims, pieces, -0.22, 0.18) if pieces else 1.0
    result = jax.random.normal(rng, dims, jnp.float32) * deviation * loudness
    return jnp.minimum(jnp.maximum(result, -reach), reach).astype(kind)


def setup_inputs(seed: int = 0) -> dict:
    streams_of = jax.random.split(jax.random.key(seed), 5)
    return {
        "activations": noise(streams_of[0], (TOKENS, D), 1.0, 6.0, ((0, 32), (1, 8))),
        "cotangent": noise(streams_of[1], (TOKENS, FF), TOKENS ** -0.5, 0.09375, ((0, 8), (1, 32))),
        "basis_in": draw_basis_in(jax.random.fold_in(streams_of[4], 71), 0),
        "basis_out": draw_basis_out(jax.random.fold_in(streams_of[4], 71), 0),
    }


def reference(activations, cotangent, basis_in, basis_out):
    highest = lax.Precision.HIGHEST
    gradient = lax.dot_general(activations, cotangent, (((0,), (0,)), ((), ())), preferred_element_type=jnp.float32)
    row_coeff = lax.dot_general(basis_in, gradient, (((0,), (0,)), ((), ())), precision=highest, preferred_element_type=jnp.float32)
    left_done = gradient - jnp.dot(basis_in, row_coeff, precision=highest, preferred_element_type=jnp.float32)
    col_coeff = jnp.dot(left_done, basis_out, precision=highest, preferred_element_type=jnp.float32)
    projected = left_done - lax.dot_general(col_coeff, basis_out, (((1,), (1,)), ((), ())), precision=highest, preferred_element_type=jnp.float32)
    return projected
```

```python
import jax
import jax.numpy as jnp
from jax import lax
from jax.experimental import pallas as pl
from jax.experimental.pallas import tpu as pltpu
from jax.sharding import Mesh, PartitionSpec as P

SIZES = {"x": 4, "l": 2, "y": 4, "h": 4, "c": 2}
IN = ("x", "l")
OUT = ("y", "h", "c")
CHIPS = ("y", "h")


def shift(value, axis, step):
    size = SIZES[axis]
    return lax.ppermute(value, axis, [(k, (k + step) % size) for k in range(size)])


def split(value):
    high = lax.reduce_precision(value, exponent_bits=8, mantissa_bits=7)
    return high.astype(jnp.bfloat16), (value - high).astype(jnp.bfloat16)


def dot(left, right, dims):
    return lax.dot_general(left, right, (dims, ((), ())), preferred_element_type=jnp.float32)


def dot_three(left, right, dims):
    lh, ll = split(left)
    rh, rl = split(right)
    return dot(lh, rh, dims) + (dot(lh, rl, dims) + dot(ll, rh, dims))


def spread(value, axes, count):
    return lax.all_to_all(jnp.broadcast_to(value, (count,) + value.shape), axes, 0, 0)


def gather_cotangent(c):
    x, l = lax.axis_index("x"), lax.axis_index("l")
    other = 1 - l
    half = c.shape[0] // 2
    left = shift(c, "x", 1)
    right = shift(c, "x", -1)
    mate = shift(c, "l", 1)
    far_top = shift(left[:half], "x", 1)
    far_low = shift(right[half:], "x", -1)
    mate_left = shift(mate, "x", 1)
    mate_right = shift(mate, "x", -1)
    mate_far_top = shift(far_top, "l", 1)
    mate_far_low = shift(far_low, "l", 1)
    whole = jnp.zeros((8,) + c.shape, c.dtype)

    def put(whole, piece, dx, lane, row=0):
        return lax.dynamic_update_slice(whole, piece[None], (((x + dx) % 4) * 2 + lane, row, 0))

    whole = put(whole, c, 0, l)
    whole = put(whole, left, -1, l)
    whole = put(whole, right, 1, l)
    whole = put(whole, mate, 0, other)
    whole = put(whole, far_top, 2, l)
    whole = put(whole, far_low, 2, l, half)
    whole = put(whole, mate_left, -1, other)
    whole = put(whole, mate_right, 1, other)
    whole = put(whole, mate_far_top, 2, other)
    whole = put(whole, mate_far_low, 2, other, half)
    return whole.reshape(-1, c.shape[1])


def gather_activations(a):
    y, core = lax.axis_index("y"), lax.axis_index("c")
    column = lax.all_gather(a, "h", axis=0)
    left = shift(column, "y", 1)
    right = shift(column, "y", -1)
    far_top = shift(left[:2], "y", 1)
    far_low = shift(right[2:], "y", -1)
    whole = jnp.zeros((4, 4, 2) + a.shape, a.dtype)

    def put(whole, piece, dy, h=0):
        twin = shift(piece, "c", 1)
        whole = lax.dynamic_update_slice(whole, piece[None, :, None], ((y + dy) % 4, h, core, 0, 0))
        return lax.dynamic_update_slice(whole, twin[None, :, None], ((y + dy) % 4, h, 1 - core, 0, 0))

    whole = put(whole, column, 0)
    whole = put(whole, left, -1)
    whole = put(whole, right, 1)
    whole = put(whole, far_top, 2)
    whole = put(whole, far_low, 2, 2)
    return whole.reshape(4096, 1024)


def encode(value):
    square = value * value
    return (square * value * jnp.abs(value)).astype(jnp.bfloat16)


def decode(code):
    wide = code.astype(jnp.float32)
    root = jnp.sqrt(jnp.sqrt(jnp.abs(wide)))
    return jnp.where(wide < 0, -root, root)


def product_kernel(a_ref, c_ref, out_ref):
    out_ref[...] = dot(a_ref[...], c_ref[...], ((0,), (0,)))


def main_product(a, c):
    return pl.pallas_call(
        product_kernel,
        grid=(4,),
        in_specs=[
            pl.BlockSpec((4096, 256), lambda i: (0, i)),
            pl.BlockSpec((4096, 896), lambda i: (0, 0), pipeline_mode=pl.Buffered(1)),
        ],
        out_specs=pl.BlockSpec((256, 896), lambda i: (i, 0)),
        out_shape=jax.ShapeDtypeStruct((1024, 896), jnp.float32),
        compiler_params=pltpu.CompilerParams(vmem_limit_bytes=40 << 20),
        cost_estimate=pl.CostEstimate(flops=2 * 1024 * 896 * 4096, bytes_accessed=20 << 20, transcendentals=0),
    )(a, c)


def final_kernel(g_ref, u_ref, r_ref, s_ref, v_ref, out_ref):
    def three(left, right, dims):
        lh = left.astype(jnp.bfloat16)
        ll = (left - lh.astype(jnp.float32)).astype(jnp.bfloat16)
        rh = right.astype(jnp.bfloat16)
        rl = (right - rh.astype(jnp.float32)).astype(jnp.bfloat16)
        return dot(lh, rh, dims) + (dot(lh, rl, dims) + dot(ll, rh, dims))

    low = three(u_ref[...], r_ref[...], ((1,), (0,)))
    out_ref[...] = g_ref[...] - (low + three(s_ref[...], v_ref[...], ((0,), (1,))))


def finish(g, u, r, s, v):
    return pl.pallas_call(
        final_kernel,
        grid=(4,),
        in_specs=[
            pl.BlockSpec((256, 896), lambda i: (i, 0)),
            pl.BlockSpec((256, 512), lambda i: (i, 0)),
            pl.BlockSpec((512, 896), lambda i: (0, 0), pipeline_mode=pl.Buffered(1)),
            pl.BlockSpec((1024, 256), lambda i: (0, i)),
            pl.BlockSpec((896, 1024), lambda i: (0, 0), pipeline_mode=pl.Buffered(1)),
        ],
        out_specs=pl.BlockSpec((256, 896), lambda i: (i, 0)),
        out_shape=jax.ShapeDtypeStruct((1024, 896), jnp.float32),
        compiler_params=pltpu.CompilerParams(vmem_limit_bytes=48 << 20),
        cost_estimate=pl.CostEstimate(flops=6 * 1024 * 896 * 1536, bytes_accessed=20 << 20, transcendentals=0),
    )(g, u, r, s, v)


def per_device(a, c, u, v):
    core = lax.axis_index("c")
    a_all = gather_activations(a)

    vh, vl = split(v)
    q = dot(vh, c, ((0,), (1,))) + dot(vl, c, ((0,), (1,)))
    mine = lax.dynamic_slice_in_dim(q, core * 512, 512, 0)
    theirs = lax.dynamic_slice_in_dim(q, 512 - core * 512, 512, 0)
    q = mine + shift(theirs, "c", 1)
    q = jnp.sum(lax.all_to_all(q.reshape(16, 32, 512), CHIPS, 0, 0), axis=0)
    q = spread(q, IN, 8)
    q = jnp.transpose(q, (1, 0, 2)).reshape(32, 4096)

    uh, ul = split(u)
    p = dot(uh, a, ((0,), (1,))) + dot(ul, a, ((0,), (1,)))
    p = jnp.sum(lax.all_to_all(p.reshape(8, 64, 128), IN, 0, 0), axis=0)
    p = spread(p, OUT, 32)
    p = jnp.transpose(p, (1, 0, 2)).reshape(64, 4096)

    t = dot_three(q, p, ((1,), (1,)))
    t = jnp.transpose(spread(t, IN, 8), (1, 0, 2)).reshape(32, 512)
    c_all = gather_cotangent(c)

    s = dot(jnp.concatenate(split(q), 0), a_all, ((1,), (0,)))
    s = s[:32] + s[32:] - dot_three(t, u, ((1,), (1,)))
    r = dot(jnp.concatenate(split(p), 0), c_all, ((1,), (0,)))
    r = r[:64] + r[64:]

    s_own = spread(encode(s), CHIPS, 16).reshape(512, 1024)
    s_other = shift(s_own, "c", 1)
    s_pair = jnp.stack([s_own, s_other])
    s_all = jnp.where(core == 0, s_pair, s_pair[::-1]).reshape(1024, 1024)
    r = spread(encode(r), IN, 8).reshape(512, 896)
    gradient = main_product(a_all, c_all)
    return finish(gradient, u, decode(r), decode(s_all), v)


def solution(mesh):
    fine = Mesh(mesh.devices.reshape(tuple(SIZES.values())), tuple(SIZES))
    placed = (P(OUT, IN), P(IN, OUT), P(IN, None), P(OUT, None))
    return jax.shard_map(per_device, mesh=fine, in_specs=placed, out_specs=P(IN, OUT), check_vma=False)
```

```python
import functools

import jax
import jax.numpy as jnp
from jax import lax
from jax.experimental import pallas as pl
from jax.experimental.pallas import tpu as pltpu
from jax.sharding import Mesh, PartitionSpec as P

SIZES = {"x": 4, "l": 2, "y": 4, "h": 4, "c": 2}
IN = ("x", "l")
OUT = ("y", "h", "c")
CHIPS = ("y", "h")
BF16, F32 = jnp.bfloat16, jnp.float32
ANY = pl.BlockSpec(memory_space=pltpu.HBM)
VMEM = pl.BlockSpec(memory_space=pltpu.VMEM)
SMEM = pl.BlockSpec(memory_space=pltpu.SMEM)
X, L, Y, H, C = range(5)


def shift(value, axis, step):
    size = SIZES[axis]
    return lax.ppermute(value, axis, [(k, (k + step) % size) for k in range(size)])


def spread(value, axes, count):
    return lax.all_to_all(jnp.broadcast_to(value, (count,) + value.shape), axes, 0, 0)


def dot(left, right, dims=((1,), (0,))):
    return lax.dot_general(left, right, (dims, ((), ())), preferred_element_type=F32)


def split(value):
    high = value.astype(BF16)
    return high, (value - high.astype(F32)).astype(BF16)


def three(left, right, dims=((1,), (0,))):
    lh, ll = split(left)
    rh, rl = split(right)
    return dot(lh, rh, dims) + (dot(lh, rl, dims) + dot(ll, rh, dims))


def encode(value):
    square = value * value
    return (square * value * jnp.abs(value)).astype(BF16)


def decode(code):
    wide = code.astype(F32)
    root = jnp.sqrt(jnp.sqrt(jnp.abs(wide)))
    return jnp.where(wide < 0, -root, root)


def call(kernel, out_shape, in_specs, scratch=(), flops=0, moved=0, **extra):
    return pl.pallas_call(
        kernel,
        out_shape=out_shape,
        in_specs=in_specs,
        out_specs=jax.tree.map(lambda _: VMEM, out_shape),
        scratch_shapes=list(scratch),
        compiler_params=pltpu.CompilerParams(vmem_limit_bytes=50 << 20),
        cost_estimate=pl.CostEstimate(flops=flops, bytes_accessed=moved, transcendentals=0),
        **extra,
    )


def shape(*dims, kind=F32):
    return jax.ShapeDtypeStruct(dims, kind)


def front_kernel(at, a_ref, c_ref, u_ref, v_ref, p_ref, mine_ref, theirs_ref):
    c = c_ref[...]
    for out_ref, which in ((theirs_ref, 1 - at[C]), (mine_ref, at[C])):
        high, low = split(v_ref[:, pl.ds(pl.multiple_of(which * 512, 512), 512)])
        out_ref[...] = (dot(c, high) + dot(c, low)).T
    high, low = split(u_ref[...])
    a = a_ref[...]
    p_ref[...] = (dot(a, high) + dot(a, low)).T


def front(at, a, c, u, v):
    return call(
        front_kernel,
        (shape(512, 128), shape(512, 512), shape(512, 512)),
        [SMEM] + [VMEM] * 4,
        flops=4 * 512 * 896 * 1024 + 4 * 128 * 1024 * 512,
        moved=10 << 20,
    )(at, a, c, u, v)


def prepare_kernel(at, v_ref, high_ref, low_ref):
    for n, which in enumerate((at[C], 1 - at[C])):
        turned = v_ref[:, pl.ds(pl.multiple_of(which * 512, 512), 512)].T
        high, low = split(turned)
        high_ref[512 * n : 512 * n + 512, :] = high
        low_ref[512 * n : 512 * n + 512, :] = low


def prepare(at, v):
    return call(
        prepare_kernel, (shape(1024, 896, kind=BF16), shape(1024, 896, kind=BF16)), [SMEM, VMEM], moved=8 << 20
    )(at, v)


def run(copies, sems):
    started = [pltpu.make_async_copy(src, dst, sems.at[k]) for k, (src, dst) in enumerate(copies)]
    for copy in started:
        copy.start()
    for copy in started:
        copy.wait()


def sems(count):
    return pltpu.SemaphoreType.DMA((count,))


def second_kernel(left, right, mate, a, p, *rest):
    xp, xm, a_out, p_out, sem = rest[-5:]
    run(
        [
            (left.at[pl.ds(0, 256)], xp.at[pl.ds(0, 256)]),
            (mate, xp.at[pl.ds(256, 512)]),
            (right.at[pl.ds(256, 256)], xm.at[pl.ds(0, 256)]),
            (mate, xm.at[pl.ds(256, 512)]),
            (a, a_out),
            (p, p_out),
        ],
        sem,
    )


def third_kernel(xp, xm, a, hp, hm, h2, *rest):
    far, column, sem = rest[-3:]
    copies = [(xp.at[pl.ds(0, 256)], far.at[pl.ds(0, 256)]), (xm.at[pl.ds(0, 256)], far.at[pl.ds(256, 256)])]
    run(copies + [(ref, column.at[k]) for k, ref in enumerate((a, hp, hm, h2))], sem)


def assemble(kernel, outs, count, operands, after):
    return pl.pallas_call(
        kernel,
        out_shape=outs,
        in_specs=[ANY] * (len(operands) + len(after)),
        out_specs=tuple(VMEM for _ in outs),
        scratch_shapes=[sems(count)],
        compiler_params=pltpu.CompilerParams(vmem_limit_bytes=50 << 20),
        cost_estimate=pl.CostEstimate(flops=0, bytes_accessed=8 << 20, transcendentals=0),
    )(*operands, *after)


def coefficients_kernel(at, q_ref, own_ref, other_ref, here_ref, there_ref, p2_ref, t_ref):
    core = at[C]
    q = jnp.concatenate([q_ref[k] for k in range(8)], axis=1)
    for b in range(16):
        one, two = q[:, 256 * b : 256 * b + 128], q[:, 256 * b + 128 : 256 * b + 256]
        where = slice(128 * b, 128 * b + 128)
        here_ref[:, where] = jnp.where(core == 0, one, two)
        there_ref[:, where] = jnp.where(core == 0, two, one)
    for n, ref in enumerate((own_ref, other_ref)):
        for k in range(16):
            high, low = split(ref[k])
            where = slice(2048 * n + 128 * k, 2048 * n + 128 * k + 128)
            p2_ref[:64, where] = high
            p2_ref[64:, where] = low
    nt = ((1,), (1,))
    t = 0.0
    for n, ref in enumerate((here_ref, there_ref)):
        where = slice(2048 * n, 2048 * n + 2048)
        qh, ql = split(ref[...])
        ph, pl_ = p2_ref[:64, where], p2_ref[64:, where]
        t = t + (dot(qh, ph, nt) + (dot(qh, pl_, nt) + dot(ql, ph, nt)))
    t_ref[...] = t


def coefficients(at, q, own, other):
    return call(
        coefficients_kernel,
        (shape(32, 2048), shape(32, 2048), shape(128, 4096, kind=BF16), shape(32, 64)),
        [SMEM] + [VMEM] * 3,
        flops=6 * 32 * 64 * 4096,
        moved=4 << 20,
    )(at, q, own, other)


CPIECES = (
    ((0, 512, 0, 0, 0),),
    ((0, 512, 0, 1, 0),),
    ((0, 512, 3, 0, 0),),
    ((0, 512, 1, 0, 0),),
    ((0, 256, 2, 0, 0), (256, 512, 3, 1, 0)),
    ((0, 256, 2, 0, 256), (256, 512, 1, 1, 0)),
    ((0, 512, 2, 1, 0),),
)


def activation_copies(at, refs, whole):
    copies = []
    for ref, dy in zip(refs, (0, 3, 1, 2)):
        for k, dh in enumerate((0, 3, 1, 2)):
            block = lax.rem(at[Y] + dy, 4) * 4 + lax.rem(at[H] + dh, 4)
            copies.append((ref.at[k], whole.at[:, pl.ds(pl.multiple_of(block * 128, 128), 128)]))
    return copies


def half_copies(at, refs, whole, core):
    copies = []
    for ref, parts in zip(refs, CPIECES):
        for row, rows, dx, dl, first in parts:
            shard = lax.rem(at[X] + dx, 4) * 2 + lax.rem(at[L] + dl, 2)
            for n in range(rows // 256):
                src = ref.at[pl.ds(pl.multiple_of(row + 256 * n + 128 * core, 128), 128)]
                dst = whole.at[pl.ds(pl.multiple_of(shard * 256 + first // 2 + 128 * n, 128), 128)]
                copies.append((src, dst))
    return copies


def s_kernel(at, here_ref, there_ref, *rest):
    refs = rest[:4]
    own_ref, other_ref, whole, sem = rest[-4:]
    run(activation_copies(at, refs, whole), sem)
    rows = jnp.concatenate(split(here_ref[...]) + split(there_ref[...]), axis=0)
    s = dot(rows, whole[...], ((1,), (1,)))
    own_ref[...] = s[:32] + s[32:64]
    other_ref[...] = s[64:96] + s[96:]


def s_parts(at, here, there, pieces, after):
    return call(
        s_kernel, (shape(32, 1024), shape(32, 1024), shape(1024, 2048, kind=BF16)),
        [SMEM] + [VMEM] * 2 + [ANY] * (4 + len(after)), (sems(16),),
        flops=2 * 128 * 2048 * 1024, moved=10 << 20,
    )(at, here, there, *pieces, *after)


def cross_kernel(t_ref, u_ref, out_ref):
    t = jnp.concatenate([t_ref[k] for k in range(8)], axis=1)
    out_ref[...] = three(t, u_ref[...], ((1,), (1,)))


def cross(t, u):
    return call(cross_kernel, shape(32, 1024), [VMEM] * 2, flops=6 * 32 * 512 * 1024, moved=3 << 20)(t, u)


def code_kernel(own_ref, other_ref, cross_ref, out_ref):
    out_ref[...] = encode(own_ref[...] + other_ref[...] - cross_ref[...])


def s_code(own, other, taken):
    return call(code_kernel, shape(32, 1024, kind=BF16), [VMEM] * 3, moved=1 << 20)(own, other, taken)


def touch_kernel(*refs):
    pass


def touch(value, after):
    return pl.pallas_call(
        touch_kernel, out_shape=shape(*value.shape, kind=value.dtype), in_specs=[ANY] * 2, out_specs=ANY,
        input_output_aliases={0: 0},
    )(value, after)


def turn_kernel(at, *rest):
    pieces, out_ref, whole = rest[:4], rest[-2], rest[-1]
    for ref, dy in zip(pieces, (0, 3, 1, 2)):
        for k, dh in enumerate((0, 3, 1, 2)):
            block = lax.rem(at[Y] + dy, 4) * 4 + lax.rem(at[H] + dh, 4)
            whole[pl.ds(pl.multiple_of(block * 32, 32), 32), :] = ref[k]
    for k in range(8):
        out_ref[128 * k : 128 * k + 128, :] = whole[:, 128 * k : 128 * k + 128].T


def turn(at, pieces, after):
    return call(
        turn_kernel, shape(1024, 512, kind=BF16), [SMEM] + [VMEM] * 4 + [ANY] * len(after),
        (pltpu.VMEM((512, 1024), BF16),), moved=3 << 20,
    )(at, *pieces, *after)


def r_kernel(at, p_ref, *rest):
    refs, (out_ref, own_ref, other_ref, sem) = rest[:7], rest[-4:]
    copies = half_copies(at, refs, own_ref, at[C]) + half_copies(at, refs, other_ref, 1 - at[C])
    run(copies, sem)
    r = dot(p_ref[:, :2048], own_ref[...]) + dot(p_ref[:, 2048:], other_ref[...])
    code = encode(r[:64] + r[64:])
    for n in range(8):
        out_ref[n] = code


def r_slices(at, p2, pieces):
    half = shape(2048, 896, kind=BF16)
    return call(
        r_kernel, (shape(8, 64, 896, kind=BF16), half, half), [SMEM, VMEM] + [ANY] * 7, (sems(32),),
        flops=2 * 128 * 4096 * 896, moved=12 << 20,
    )(at, p2, *pieces)


def final_kernel(g_ref, u_ref, r_ref, own_ref, other_ref, high_ref, low_ref, out_ref, rh_ref, rl_ref):
    @pl.when(pl.program_id(0) == 0)
    def _():
        high, low = split(decode(r_ref[...]))
        rh_ref[:512, :] = high
        rl_ref[:512, :] = low
        rh_ref[512:, :] = high_ref[...]
        rl_ref[512:, :] = low_ref[...]

    parts = [u_ref[...], decode(own_ref[...]), decode(other_ref[...])]
    highs, lows = zip(*map(split, parts))
    high, low = jnp.concatenate(highs, axis=1), jnp.concatenate(lows, axis=1)
    out_ref[...] = g_ref[...] - (dot(high, rh_ref[...]) + (dot(high, rl_ref[...]) + dot(low, rh_ref[...])))


def final(g, u, r, own, other, high, low):
    def rows(width):
        return pl.BlockSpec((512, width), lambda k: (k, 0))

    def whole(height):
        return pl.BlockSpec((height, 896), lambda k: (0, 0), pipeline_mode=pl.Buffered(1))

    return pl.pallas_call(
        final_kernel,
        grid=(2,),
        in_specs=[rows(896), rows(512), whole(512), rows(512), rows(512), whole(1024), whole(1024)],
        out_specs=rows(896),
        out_shape=shape(1024, 896),
        scratch_shapes=[pltpu.VMEM((1536, 896), BF16)] * 2,
        compiler_params=pltpu.CompilerParams(vmem_limit_bytes=50 << 20),
        cost_estimate=pl.CostEstimate(flops=6 * 1024 * 896 * 1536, bytes_accessed=16 << 20, transcendentals=0),
    )(g, u, r, own, other, high, low)


def add_up(parts):
    return jnp.sum(parts, axis=0)


def per_device(a, c, u, v):
    at = jnp.stack([lax.axis_index(n) for n in SIZES]).astype(jnp.int32)
    a_turned = a.T
    left, right, mate = shift(c, "x", 1), shift(c, "x", -1), shift(c, "l", 1)
    p, mine, theirs = front(at, a, c, u, v)
    q = mine + shift(theirs, "c", 1)
    q = add_up(lax.all_to_all(q.reshape(4, 128, 512), "y", 0, 0))

    strip = shape(768, 896, kind=BF16)
    xp, xm, a_turned, p = assemble(
        second_kernel, (strip, strip, shape(1024, 128, kind=BF16), shape(512, 128)), 6,
        (left, right, mate, a_turned, p), (q,),
    )
    xp, xm = shift(xp, "x", 1), shift(xm, "x", -1)
    hp, hm, h2 = shift(a_turned, "h", 1), shift(a_turned, "h", -1), shift(a_turned, "h", 2)
    p = add_up(lax.all_to_all(p.reshape(8, 64, 128), IN, 0, 0))
    q = add_up(lax.all_to_all(q.reshape(4, 32, 512), "h", 0, 0))

    far, column = assemble(
        third_kernel, (shape(512, 896, kind=BF16), shape(4, 1024, 128, kind=BF16)), 6,
        (xp, xm, a_turned, hp, hm, h2), (q, p),
    )
    far = shift(far, "l", 1)
    apieces = [column] + [shift(column, "y", step) for step in (1, -1, 2)]
    q = spread(q, IN, 8)
    p_own = spread(p, CHIPS, 16)
    here, there, p2, t = coefficients(at, q, p_own, shift(p_own, "c", 1))
    there = shift(there, "c", 1)
    taken = cross(spread(t, IN, 8), u)
    vh, vl = prepare(at, v)
    r, c_own, c_other = r_slices(at, p2, (c, mate, left, right, xp, xm, far))
    r = lax.all_to_all(r, IN, 0, 0).reshape(512, 896)

    s, s_other, a_own = s_parts(at, here, there, apieces, (taken, vh, c_own))
    s = s_code(s, shift(s_other, "c", 1), taken)
    a_own = touch(a_own, s)
    column = jnp.stack([s, shift(s, "h", 1), shift(s, "h", -1), shift(s, "h", 2)])
    spieces = [column] + [shift(column, "y", step) for step in (1, -1, 2)]
    g = dot(a_own, c_own) + dot(shift(a_own, "c", 1), c_other)
    s = turn(at, spieces, (g, r))
    return final(g, u, r, s, shift(s, "c", 1), vh, vl)


def solution(mesh):
    fine = Mesh(mesh.devices.reshape(tuple(SIZES.values())), tuple(SIZES))
    placed = (P(OUT, IN), P(IN, OUT), P(IN, None), P(OUT, None))
    return jax.shard_map(per_device, mesh=fine, in_specs=placed, out_specs=P(IN, OUT), check_vma=False)
```

```python
import functools

import jax
import jax.numpy as jnp
from jax import lax
from jax.experimental import pallas as pl
from jax.experimental.pallas import tpu as pltpu
from jax.sharding import Mesh, PartitionSpec as P

SIZES = {"x": 4, "l": 2, "y": 4, "h": 4, "c": 2}
IN = ("x", "l")
OUT = ("y", "h", "c")
CHIPS = ("y", "h")
BF16, F32 = jnp.bfloat16, jnp.float32
ANY = pl.BlockSpec(memory_space=pltpu.HBM)
VMEM = pl.BlockSpec(memory_space=pltpu.VMEM)
SMEM = pl.BlockSpec(memory_space=pltpu.SMEM)
X, L, Y, H, C = range(5)


def shift(value, axis, step):
    size = SIZES[axis]
    return lax.ppermute(value, axis, [(k, (k + step) % size) for k in range(size)])


def spread(value, axes, count):
    return lax.all_to_all(jnp.broadcast_to(value, (count,) + value.shape), axes, 0, 0)


def dot(left, right, dims=((1,), (0,))):
    return lax.dot_general(left, right, (dims, ((), ())), preferred_element_type=F32)


def split(value):
    high = value.astype(BF16)
    return high, (value - high.astype(F32)).astype(BF16)


def three(left, right, dims=((1,), (0,))):
    lh, ll = split(left)
    rh, rl = split(right)
    return dot(lh, rh, dims) + (dot(lh, rl, dims) + dot(ll, rh, dims))


def encode(value):
    square = value * value
    return (square * value * jnp.abs(value)).astype(BF16)


def decode(code):
    wide = code.astype(F32)
    root = lax.rsqrt(lax.rsqrt(jnp.abs(wide)))
    return jnp.where(wide < 0, -root, jnp.where(wide > 0, root, 0.0))


def call(kernel, out_shape, in_specs, scratch=(), flops=0, moved=0, **extra):
    return pl.pallas_call(
        kernel,
        out_shape=out_shape,
        in_specs=in_specs,
        out_specs=jax.tree.map(lambda _: VMEM, out_shape),
        scratch_shapes=list(scratch),
        compiler_params=pltpu.CompilerParams(vmem_limit_bytes=50 << 20),
        cost_estimate=pl.CostEstimate(flops=flops, bytes_accessed=moved, transcendentals=0),
        **extra,
    )


def shape(*dims, kind=F32):
    return jax.ShapeDtypeStruct(dims, kind)


def front_kernel(at, a_ref, c_ref, u_ref, v_ref, p_ref, mine_ref, theirs_ref):
    c = c_ref[...]
    for out_ref, which in ((theirs_ref, 1 - at[C]), (mine_ref, at[C])):
        high, low = split(v_ref[:, pl.ds(pl.multiple_of(which * 512, 512), 512)])
        out_ref[...] = (dot(c, high) + dot(c, low)).T
    high, low = split(u_ref[...])
    a = a_ref[...]
    p_ref[...] = (dot(a, high) + dot(a, low)).T


def front(at, a, c, u, v):
    return call(
        front_kernel,
        (shape(512, 128), shape(512, 512), shape(512, 512)),
        [SMEM] + [VMEM] * 4,
        flops=4 * 512 * 896 * 1024 + 4 * 128 * 1024 * 512,
        moved=10 << 20,
    )(at, a, c, u, v)


def prepare_kernel(at, v_ref, u_ref, high_ref, low_ref, uh_ref, ul_ref):
    uh_ref[...], ul_ref[...] = split(u_ref[...])
    for n, which in enumerate((at[C], 1 - at[C])):
        turned = v_ref[:, pl.ds(pl.multiple_of(which * 512, 512), 512)].T
        high, low = split(turned)
        high_ref[512 * n : 512 * n + 512, :] = high
        low_ref[512 * n : 512 * n + 512, :] = low


def prepare(at, v, u):
    tall, wide = shape(1024, 896, kind=BF16), shape(1024, 512, kind=BF16)
    return call(prepare_kernel, (tall, tall, wide, wide), [SMEM, VMEM, VMEM], moved=12 << 20)(at, v, u)


def run(copies, sems):
    started = [pltpu.make_async_copy(src, dst, sems.at[k]) for k, (src, dst) in enumerate(copies)]
    for copy in started:
        copy.start()
    for copy in started:
        copy.wait()


def sems(count):
    return pltpu.SemaphoreType.DMA((count,))


def second_kernel(left, right, mate, a, p, *rest):
    xp, xm, a_out, p_out, sem = rest[-5:]
    run(
        [
            (left.at[pl.ds(0, 256)], xp.at[pl.ds(0, 256)]),
            (mate, xp.at[pl.ds(256, 512)]),
            (right.at[pl.ds(256, 256)], xm.at[pl.ds(0, 256)]),
            (mate, xm.at[pl.ds(256, 512)]),
            (a, a_out),
            (p, p_out),
        ],
        sem,
    )


def third_kernel(xp, xm, a, hp, hm, h2, *rest):
    far, column, sem = rest[-3:]
    copies = [(xp.at[pl.ds(0, 256)], far.at[pl.ds(0, 256)]), (xm.at[pl.ds(0, 256)], far.at[pl.ds(256, 256)])]
    run(copies + [(ref, column.at[k]) for k, ref in enumerate((a, hp, hm, h2))], sem)


def assemble(kernel, outs, count, operands, after):
    return pl.pallas_call(
        kernel,
        out_shape=outs,
        in_specs=[ANY] * (len(operands) + len(after)),
        out_specs=tuple(VMEM for _ in outs),
        scratch_shapes=[sems(count)],
        compiler_params=pltpu.CompilerParams(vmem_limit_bytes=50 << 20),
        cost_estimate=pl.CostEstimate(flops=0, bytes_accessed=8 << 20, transcendentals=0),
    )(*operands, *after)


def coefficients_kernel(at, q_ref, own_ref, other_ref, here_ref, there_ref, p2_ref, t_ref):
    core = at[C]
    q = jnp.concatenate([q_ref[k] for k in range(8)], axis=1)
    for b in range(16):
        one, two = q[:, 256 * b : 256 * b + 128], q[:, 256 * b + 128 : 256 * b + 256]
        where = slice(128 * b, 128 * b + 128)
        here_ref[:, where] = jnp.where(core == 0, one, two)
        there_ref[:, where] = jnp.where(core == 0, two, one)
    for n, ref in enumerate((own_ref, other_ref)):
        for k in range(16):
            high, low = split(ref[k])
            where = slice(2048 * n + 128 * k, 2048 * n + 128 * k + 128)
            p2_ref[:64, where] = high
            p2_ref[64:, where] = low
    nt = ((1,), (1,))
    t = 0.0
    for n, ref in enumerate((here_ref, there_ref)):
        where = slice(2048 * n, 2048 * n + 2048)
        qh, ql = split(ref[...])
        ph, pl_ = p2_ref[:64, where], p2_ref[64:, where]
        t = t + (dot(qh, ph, nt) + (dot(qh, pl_, nt) + dot(ql, ph, nt)))
    t_ref[...] = t


def coefficients(at, q, own, other):
    return call(
        coefficients_kernel,
        (shape(32, 2048), shape(32, 2048), shape(128, 4096, kind=BF16), shape(32, 64)),
        [SMEM] + [VMEM] * 3,
        flops=6 * 32 * 64 * 4096,
        moved=4 << 20,
    )(at, q, own, other)


CPIECES = (
    ((0, 512, 0, 0, 0),),
    ((0, 512, 0, 1, 0),),
    ((0, 512, 3, 0, 0),),
    ((0, 512, 1, 0, 0),),
    ((0, 256, 2, 0, 0), (256, 512, 3, 1, 0)),
    ((0, 256, 2, 0, 256), (256, 512, 1, 1, 0)),
    ((0, 512, 2, 1, 0),),
)


def activation_copies(at, refs, whole):
    copies = []
    for ref, dy in zip(refs, (0, 3, 1, 2)):
        for k, dh in enumerate((0, 3, 1, 2)):
            block = lax.rem(at[Y] + dy, 4) * 4 + lax.rem(at[H] + dh, 4)
            copies.append((ref.at[k], whole.at[:, pl.ds(pl.multiple_of(block * 128, 128), 128)]))
    return copies


def half_copies(at, refs, whole, core):
    copies = []
    for ref, parts in zip(refs, CPIECES):
        for row, rows, dx, dl, first in parts:
            shard = lax.rem(at[X] + dx, 4) * 2 + lax.rem(at[L] + dl, 2)
            for n in range(rows // 256):
                src = ref.at[pl.ds(pl.multiple_of(row + 256 * n + 128 * core, 128), 128)]
                dst = whole.at[pl.ds(pl.multiple_of(shard * 256 + first // 2 + 128 * n, 128), 128)]
                copies.append((src, dst))
    return copies


def s_kernel(at, here_ref, there_ref, *rest):
    refs = rest[:4]
    own_ref, other_ref, whole, sem = rest[-4:]
    run(activation_copies(at, refs, whole), sem)
    rows = jnp.concatenate(split(here_ref[...]) + split(there_ref[...]), axis=0)
    s = dot(rows, whole[...], ((1,), (1,)))
    own_ref[...] = s[:32] + s[32:64]
    other_ref[...] = s[64:96] + s[96:]


def s_parts(at, here, there, pieces, after):
    return call(
        s_kernel, (shape(32, 1024), shape(32, 1024), shape(1024, 2048, kind=BF16)),
        [SMEM] + [VMEM] * 2 + [ANY] * (4 + len(after)), (sems(16),),
        flops=2 * 128 * 2048 * 1024, moved=10 << 20,
    )(at, here, there, *pieces, *after)


def cross_kernel(t_ref, u_ref, out_ref):
    t = jnp.concatenate([t_ref[k] for k in range(8)], axis=1)
    out_ref[...] = three(t, u_ref[...], ((1,), (1,)))


def cross(t, u):
    return call(cross_kernel, shape(32, 1024), [VMEM] * 2, flops=6 * 32 * 512 * 1024, moved=3 << 20)(t, u)


def code_kernel(own_ref, other_ref, cross_ref, out_ref):
    out_ref[...] = encode(own_ref[...] + other_ref[...] - cross_ref[...])


def s_code(own, other, taken):
    return call(code_kernel, shape(32, 1024, kind=BF16), [VMEM] * 3, moved=1 << 20)(own, other, taken)


def touch_kernel(*refs):
    pass


def touch(value, after):
    return pl.pallas_call(
        touch_kernel, out_shape=shape(*value.shape, kind=value.dtype), in_specs=[ANY] * 2, out_specs=ANY,
        input_output_aliases={0: 0},
    )(value, after)


def turn_kernel(at, *rest):
    pieces, out_ref, whole = rest[:4], rest[-2], rest[-1]
    for ref, dy in zip(pieces, (0, 3, 1, 2)):
        for k, dh in enumerate((0, 3, 1, 2)):
            block = lax.rem(at[Y] + dy, 4) * 4 + lax.rem(at[H] + dh, 4)
            whole[pl.ds(pl.multiple_of(block * 32, 32), 32), :] = ref[k]
    for k in range(8):
        out_ref[128 * k : 128 * k + 128, :] = whole[:, 128 * k : 128 * k + 128].T


def turn(at, pieces, after):
    return call(
        turn_kernel, shape(1024, 512, kind=BF16), [SMEM] + [VMEM] * 4 + [ANY] * len(after),
        (pltpu.VMEM((512, 1024), BF16),), moved=3 << 20,
    )(at, *pieces, *after)


def r_kernel(at, p_ref, *rest):
    refs, (out_ref, own_ref, other_ref, sem) = rest[:7], rest[-4:]
    copies = half_copies(at, refs, own_ref, at[C]) + half_copies(at, refs, other_ref, 1 - at[C])
    run(copies, sem)
    r = dot(p_ref[:, :2048], own_ref[...]) + dot(p_ref[:, 2048:], other_ref[...])
    code = encode(r[:64] + r[64:])
    for n in range(8):
        out_ref[n] = code


def r_slices(at, p2, pieces):
    half = shape(2048, 896, kind=BF16)
    return call(
        r_kernel, (shape(8, 64, 896, kind=BF16), half, half), [SMEM, VMEM] + [ANY] * 7, (sems(32),),
        flops=2 * 128 * 4096 * 896, moved=12 << 20,
    )(at, p2, *pieces)


def final_kernel(g_ref, uh_ref, ul_ref, r_ref, own_ref, other_ref, high_ref, low_ref, out_ref, rh_ref, rl_ref):
    @pl.when(pl.program_id(0) == 0)
    def _():
        high, low = split(decode(r_ref[...]))
        rh_ref[:512, :] = high
        rl_ref[:512, :] = low
        rh_ref[512:, :] = high_ref[...]
        rl_ref[512:, :] = low_ref[...]

    own_high, own_low = split(decode(own_ref[...]))
    other_high, other_low = split(decode(other_ref[...]))
    high = jnp.concatenate([uh_ref[...], own_high, other_high], axis=1)
    low = jnp.concatenate([ul_ref[...], own_low, other_low], axis=1)
    out_ref[...] = g_ref[...] - (dot(high, rh_ref[...]) + (dot(high, rl_ref[...]) + dot(low, rh_ref[...])))


def final(g, uh, ul, r, own, other, high, low):
    def rows(width):
        return pl.BlockSpec((512, width), lambda k: (k, 0))

    def whole(height):
        return pl.BlockSpec((height, 896), lambda k: (0, 0), pipeline_mode=pl.Buffered(1))

    return pl.pallas_call(
        final_kernel,
        grid=(2,),
        in_specs=[rows(896), rows(512), rows(512), whole(512), rows(512), rows(512), whole(1024), whole(1024)],
        out_specs=rows(896),
        out_shape=shape(1024, 896),
        scratch_shapes=[pltpu.VMEM((1536, 896), BF16)] * 2,
        compiler_params=pltpu.CompilerParams(vmem_limit_bytes=50 << 20),
        cost_estimate=pl.CostEstimate(flops=6 * 1024 * 896 * 1536, bytes_accessed=16 << 20, transcendentals=0),
    )(g, uh, ul, r, own, other, high, low)


def add_up(parts):
    return jnp.sum(parts, axis=0)


def per_device(a, c, u, v):
    at = jnp.stack([lax.axis_index(n) for n in SIZES]).astype(jnp.int32)
    a_turned = a.T
    left, right, mate = shift(c, "x", 1), shift(c, "x", -1), shift(c, "l", 1)
    p, mine, theirs = front(at, a, c, u, v)
    q = mine + shift(theirs, "c", 1)
    q = add_up(lax.all_to_all(q.reshape(4, 128, 512), "y", 0, 0))

    strip = shape(768, 896, kind=BF16)
    xp, xm, a_turned, p = assemble(
        second_kernel, (strip, strip, shape(1024, 128, kind=BF16), shape(512, 128)), 6,
        (left, right, mate, a_turned, p), (q,),
    )
    xp, xm = shift(xp, "x", 1), shift(xm, "x", -1)
    hp, hm, h2 = shift(a_turned, "h", 1), shift(a_turned, "h", -1), shift(a_turned, "h", 2)
    p = add_up(lax.all_to_all(p.reshape(8, 64, 128), IN, 0, 0))
    q = add_up(lax.all_to_all(q.reshape(4, 32, 512), "h", 0, 0))

    far, column = assemble(
        third_kernel, (shape(512, 896, kind=BF16), shape(4, 1024, 128, kind=BF16)), 6,
        (xp, xm, a_turned, hp, hm, h2), (q, p),
    )
    far = shift(far, "l", 1)
    apieces = [column] + [shift(column, "y", step) for step in (1, -1, 2)]
    q = spread(q, IN, 8)
    p_own = spread(p, CHIPS, 16)
    here, there, p2, t = coefficients(at, q, p_own, shift(p_own, "c", 1))
    there = shift(there, "c", 1)
    taken = cross(spread(t, IN, 8), u)
    vh, vl, uh, ul = prepare(at, v, u)
    r, c_own, c_other = r_slices(at, p2, (c, mate, left, right, xp, xm, far))
    r = lax.all_to_all(r, IN, 0, 0).reshape(512, 896)

    s, s_other, a_own = s_parts(at, here, there, apieces, (taken, vh, c_own))
    s = s_code(s, shift(s_other, "c", 1), taken)
    a_own = touch(a_own, s)
    column = jnp.stack([s, shift(s, "h", 1), shift(s, "h", -1), shift(s, "h", 2)])
    spieces = [column] + [shift(column, "y", step) for step in (1, -1, 2)]
    g = dot(a_own, c_own) + dot(shift(a_own, "c", 1), c_other)
    s = turn(at, spieces, (g, r))
    return final(g, uh, ul, r, s, shift(s, "c", 1), vh, vl)


def solution(mesh):
    fine = Mesh(mesh.devices.reshape(tuple(SIZES.values())), tuple(SIZES))
    placed = (P(OUT, IN), P(IN, OUT), P(IN, None), P(OUT, None))
    return jax.shard_map(per_device, mesh=fine, in_specs=placed, out_specs=P(IN, OUT), check_vma=False)
```
